128 devices in a mesh: dp: 16 (over z_hi, y, core), blk: 8 (over x, z_lo).
Axes of the slice: x: 4, y: 4, z: 4 (z_hi: 2, z_lo: 2; z = z_hi * 2 + z_lo), core: 2. Of those that a mesh axis runs over, the one named last changes fastest.
Arguments:
- queries: bfloat16 [24576, 4096], P(('dp', 'blk')), parts along dimension 0
- keys: bfloat16 [24576, 1024], P(('dp', 'blk')), parts along dimension 0
- values: bfloat16 [24576, 1024], P(('dp', 'blk')), parts along dimension 0, may hold values from -6 to 6
- outputs: bfloat16 [24576, 4096], P(('dp', 'blk')), parts along dimension 0, may hold values from -3 to 3
- output_gradient: bfloat16 [24576, 4096], P(('dp', 'blk')), parts along dimension 0, may hold values from -6 to 6
- doc_ids: int32 [24576], P(('dp', 'blk')), parts along dimension 0, may hold values from 0 to 7, as said below
Outputs:
- query_grad: bfloat16 [24576, 4096], P(('dp', 'blk')), parts along dimension 0
- gradient_of_keys: bfloat16 [24576, 1024], P(('dp', 'blk')), parts along dimension 0
- gradient_of_values: bfloat16 [24576, 1024], P(('dp', 'blk')), parts along dimension 0
The draws below stay inside these ranges and needn't reach their ends.
There are 16 independent parts, one for each index of `dp`. The reference program is written for one: setup_inputs(seed, part) draws one part's arguments, and reference() takes and returns one part's arrays. A program takes and returns all parts, laid end to end along the dimension named above; each array names one. Nothing has to cross between parts.
Inputs may be any that keep to these rules, and one draw needn't show every extreme that they name: `doc_ids`: document numbers never fall along the sequence; every document holds at most 768 tokens and one holds exactly 768.
All inputs are finite; a program needn't handle non-finite values.
Results may differ from the reference program's by a relative error of at most 0.007.
Values may be sent and summed in bfloat16 or wider, within the bound.
No kernel may reach another device: no remote copies, remote signals or barrier semaphores. Data moves between devices by JAX's collectives and lax.ppermute only.
A program may use at most 192 MiB of HBM per device.

```python
import math
import jax
import jax.numpy as jnp
from jax import lax

QUERY_HEADS = 32
KEY_VALUE_HEADS = 8
HEAD_WIDTH = 128
TOK_DEV = 192
PACKED_TOKENS = 1536
MOST = 768
DOCS = 8


def drawn_parts(key):
    starting_keys = jax.random.normal(jax.random.fold_in(key, 101), (PACKED_TOKENS, KEY_VALUE_HEADS * HEAD_WIDTH), jnp.float32)
    return starting_keys


def draw_keys(key, part):
    starting_keys = drawn_parts(key)
    return starting_keys.astype(jnp.bfloat16)


def draw_queries(key, part):
    key = jax.random.fold_in(key, 2)
    fresh = jax.random.normal(key, (PACKED_TOKENS, QUERY_HEADS * HEAD_WIDTH), jnp.float32)
    return fresh.astype(jnp.bfloat16)


def draw_doc_ids(key, part):
    key = jax.random.fold_in(key, 7)
    first_length = jax.random.randint(key, (), 1, TOK_DEV).astype(jnp.int32)
    token_index = jnp.arange(PACKED_TOKENS, dtype=jnp.int32)
    remaining = PACKED_TOKENS - first_length - MOST
    later = token_index - first_length - MOST
    later_doc = 2 + jnp.maximum(later, 0) * (DOCS - 2) // remaining
    return jnp.where(token_index < first_length, 0, jnp.where(later < 0, 1, later_doc)).astype(jnp.int32)


def levels(rng, shape, pieces, low, top_value):
    level, own = 1.0, jax.random.fold_in(rng, 6)
    for axis_at, parts in pieces:
        steps = jnp.exp(jax.random.uniform(jax.random.fold_in(own, axis_at), (parts,), jnp.float32, low / len(pieces), top_value / len(pieces)))
        level = level * jnp.repeat(steps, shape[axis_at] // parts).reshape([-1 if axis == axis_at else 1 for axis in range(len(shape))])
    return level


def normal_values(own_key, extent, spread, reach, split=(), held_as=jnp.bfloat16):
    factor_of = levels(own_key, extent, split, -0.22, 0.18) if split else 1.0
    entries = jax.random.normal(own_key, extent, jnp.float32) * spread * factor_of
    return jnp.minimum(jnp.maximum(entries, -reach), reach).astype(held_as)


def setup_inputs(seed: int = 0, part: int = 0) -> dict:
    streams_of = jax.random.split(jax.random.key(seed), 7)
    own_keys = jax.random.split(jax.random.fold_in(streams_of[6], part), 7)
    return {
        "queries": draw_queries(jax.random.fold_in(jax.random.fold_in(streams_of[6], part), 71), part),
        "keys": draw_keys(jax.random.fold_in(jax.random.fold_in(streams_of[6], part), 71), part),
        "values": normal_values(own_keys[2], (PACKED_TOKENS, KEY_VALUE_HEADS * HEAD_WIDTH), 1.0, 6.0, ((0, 8),)),
        "outputs": normal_values(own_keys[3], (PACKED_TOKENS, QUERY_HEADS * HEAD_WIDTH), 0.5, 3.0, ((0, 8),)),
        "output_gradient": normal_values(own_keys[4], (PACKED_TOKENS, QUERY_HEADS * HEAD_WIDTH), 1.0, 6.0, ((0, 8),)),
        "doc_ids": draw_doc_ids(jax.random.fold_in(jax.random.fold_in(streams_of[6], part), 71), part),
    }


def reference(queries, keys, values, outputs, output_gradient, doc_ids):
    group_width = QUERY_HEADS // KEY_VALUE_HEADS
    scale_for_scores = 1.0 / math.sqrt(HEAD_WIDTH)
    positions = jnp.arange(PACKED_TOKENS, dtype=jnp.int32)
    allowed = (doc_ids[:, None] == doc_ids[None, :]) & (positions[None, :] <= positions[:, None])
    head_queries = queries.reshape(PACKED_TOKENS, QUERY_HEADS, HEAD_WIDTH).transpose(1, 0, 2)
    output_heads = outputs.reshape(PACKED_TOKENS, QUERY_HEADS, HEAD_WIDTH).transpose(1, 0, 2)
    gradient_head_rows = output_gradient.reshape(PACKED_TOKENS, QUERY_HEADS, HEAD_WIDTH).transpose(1, 0, 2)
    head_keys = jnp.repeat(keys.reshape(PACKED_TOKENS, KEY_VALUE_HEADS, HEAD_WIDTH).transpose(1, 0, 2), group_width, axis=0)
    head_values = jnp.repeat(values.reshape(PACKED_TOKENS, KEY_VALUE_HEADS, HEAD_WIDTH).transpose(1, 0, 2), group_width, axis=0)

    def per_head(inputs):
        q_head, k_head, v_head, o_head, g_head = inputs
        scores = jnp.dot(q_head, k_head.T, preferred_element_type=jnp.float32) * scale_for_scores
        masked = jnp.where(allowed, scores, -1e+30)
        row_max = lax.optimization_barrier(jnp.max(masked, axis=1))
        total = lax.optimization_barrier(jnp.sum(jnp.where(allowed, jnp.exp(masked - row_max[:, None]), 0.0), axis=1))
        lse = row_max + jnp.log(total)
        probs = jnp.exp(jnp.where(allowed, scores - lse[:, None], -1e+30))
        probs_low = probs.astype(jnp.bfloat16)
        row_delta = lax.optimization_barrier(jnp.sum(g_head.astype(jnp.float32) * o_head.astype(jnp.float32), axis=1))
        value_part = jnp.dot(probs_low.T, g_head, preferred_element_type=jnp.float32)
        prob_grad = jnp.dot(g_head, v_head.T, preferred_element_type=jnp.float32)
        score_grad = (probs * (prob_grad - row_delta[:, None])).astype(jnp.bfloat16)
        query_part = jnp.dot(score_grad, k_head, preferred_element_type=jnp.float32)
        key_part = jnp.dot(score_grad.T, q_head, preferred_element_type=jnp.float32)
        return (query_part, key_part, value_part)
    query_parts, key_pieces_list, value_pieces_list = lax.map(per_head, (head_queries, head_keys, head_values, output_heads, gradient_head_rows))
    query_grad = (query_parts * scale_for_scores).transpose(1, 0, 2).reshape(PACKED_TOKENS, QUERY_HEADS * HEAD_WIDTH).astype(jnp.bfloat16)
    summed_key_gradient = key_pieces_list.reshape(KEY_VALUE_HEADS, group_width, PACKED_TOKENS, HEAD_WIDTH).sum(axis=1) * scale_for_scores
    summed_value_gradient = value_pieces_list.reshape(KEY_VALUE_HEADS, group_width, PACKED_TOKENS, HEAD_WIDTH).sum(axis=1)
    gradient_of_keys = summed_key_gradient.transpose(1, 0, 2).reshape(PACKED_TOKENS, KEY_VALUE_HEADS * HEAD_WIDTH).astype(jnp.bfloat16)
    gradient_of_values = summed_value_gradient.transpose(1, 0, 2).reshape(PACKED_TOKENS, KEY_VALUE_HEADS * HEAD_WIDTH).astype(jnp.bfloat16)
    return (query_grad, gradient_of_keys, gradient_of_values)
```

```python
import math

import jax
import jax.numpy as jnp
from jax import lax
from jax.experimental import pallas as pl
from jax.experimental.pallas import tpu as pltpu
from jax.sharding import PartitionSpec as P

QUERY_HEADS = 32
KEY_VALUE_HEADS = 8
HEAD_WIDTH = 128
GROUP = QUERY_HEADS // KEY_VALUE_HEADS
DOCS = 8
TOK = 192
BLOCKS = 8
MOST_BLOCKS = 5
PAIR = 2 * TOK
Q_AT = 0
G_AT = GROUP * TOK
K_AT = 2 * GROUP * TOK
V_AT = K_AT + TOK
X_AT = V_AT + TOK
SEND_ROWS = X_AT + 16
BACK_ROWS = (GROUP + 2) * TOK
NT = (((1,), (1,)), ((), ()))
TN = (((0,), (0,)), ((), ()))
NN = (((1,), (0,)), ((), ()))


def dot(a, b, dims):
    return lax.dot_general(a, b, dims, preferred_element_type=jnp.float32)


def rows_of(flat):
    return jnp.concatenate(
        [flat[:, t * 128 : (t + 1) * 128] for t in range(flat.shape[1] // 128)], axis=0
    )


def pack_kernel(q_ref, k_ref, v_ref, o_ref, g_ref, doc_ref, out_ref):
    product = []
    for h in range(GROUP):
        cols = slice(h * HEAD_WIDTH, (h + 1) * HEAD_WIDTH)
        g = g_ref[:, cols]
        out_ref[0, Q_AT + h * TOK : Q_AT + (h + 1) * TOK, :] = q_ref[:, cols]
        out_ref[0, G_AT + h * TOK : G_AT + (h + 1) * TOK, :] = g
        product.append(g.astype(jnp.float32) * o_ref[:, cols].astype(jnp.float32))
    out_ref[0, K_AT : K_AT + TOK, :] = k_ref[...]
    out_ref[0, V_AT : V_AT + TOK, :] = v_ref[...]
    delta = jnp.sum(jnp.concatenate(product, axis=0).T, axis=0, keepdims=True)
    delta = rows_of(delta)
    high = delta.astype(jnp.bfloat16).astype(jnp.float32)
    extra = jnp.concatenate(
        [high, delta - high, doc_ref[...], jnp.zeros((1, 128), jnp.float32)], axis=0
    )
    out_ref[0, X_AT : X_AT + 16, :] = extra.astype(jnp.bfloat16)


def attention_kernel(pay_ref, out_ref, extra_ref, start_ref, first_ref, dk_ref, dv_ref):
    scale = 1.0 / math.sqrt(HEAD_WIDTH)
    to_exp2 = scale * math.log2(math.e)
    dk_ref[...] = jnp.zeros_like(dk_ref)
    dv_ref[...] = jnp.zeros_like(dv_ref)
    for b in range(BLOCKS):
        extra_ref[b] = pay_ref[b, X_AT : X_AT + 16, :].astype(jnp.float32)
    docs = jnp.concatenate([extra_ref[b, 12:15, :] for b in range(BLOCKS)], axis=0)
    starts = jnp.zeros_like(docs)
    for d in range(1, DOCS):
        before = 0.5 * jnp.sum(jnp.where(docs < d, 1.0, 0.0), keepdims=True)
        starts = jnp.where(docs == d, before, starts)
    for b in range(BLOCKS):
        own = starts[3 * b : 3 * b + 3]
        start_ref[b] = jnp.concatenate([own, own, own[:2]], axis=0)
        first_ref[b] = jnp.min(own).astype(jnp.int32)

    def query_block(i, carry):
        first_block = first_ref[i] // TOK
        first_row = start_ref[i]
        start = jnp.concatenate([first_row[t : t + 1] for t in range(3)], axis=1).astype(jnp.int32)
        lane = lax.broadcasted_iota(jnp.int32, (1, PAIR), 1)
        query_pos = jnp.where(lane >= TOK, lane - TOK, lane) + i * TOK
        delta6 = extra_ref[i, 0:6, :] + extra_ref[i, 6:12, :]

        def with_blocks(count):
            low = i - count + 1
            rows = count * TOK
            keys = pay_ref[pl.ds(low, count), K_AT : K_AT + TOK, :].reshape(rows, HEAD_WIDTH)
            values = pay_ref[pl.ds(low, count), V_AT : V_AT + TOK, :].reshape(rows, HEAD_WIDTH)
            key_pos = lax.broadcasted_iota(jnp.int32, (rows, PAIR), 0) + low * TOK
            allowed = (key_pos >= start) & (key_pos <= query_pos)
            dk = jnp.zeros((rows, HEAD_WIDTH), jnp.float32)
            dv = jnp.zeros((rows, HEAD_WIDTH), jnp.float32)
            for pair in range(GROUP // 2):
                q = pay_ref[i, Q_AT + pair * PAIR : Q_AT + (pair + 1) * PAIR, :]
                g = pay_ref[i, G_AT + pair * PAIR : G_AT + (pair + 1) * PAIR, :]
                delta = jnp.concatenate(
                    [delta6[3 * pair + t : 3 * pair + t + 1] for t in range(3)], axis=1
                )
                scores = jnp.where(allowed, dot(keys, q, NT), -1e30)
                top = jnp.max(scores, axis=0, keepdims=True)
                weights = jnp.exp2(scores * to_exp2 - top * to_exp2)
                total = jnp.sum(weights, axis=0, keepdims=True)
                probs = weights * (1.0 / total)
                dv = dv + dot(probs.astype(jnp.bfloat16), g, NN)
                prob_grad = dot(values, g, NT)
                score_grad = (probs * (prob_grad - delta)).astype(jnp.bfloat16)
                dk = dk + dot(score_grad, q, NN)
                dq = dot(score_grad, keys, TN) * scale
                out_ref[i, pair * PAIR : (pair + 1) * PAIR, :] = dq.astype(jnp.bfloat16)
            dk_ref[pl.ds(low, count)] += dk.reshape(count, TOK, HEAD_WIDTH)
            dv_ref[pl.ds(low, count)] += dv.reshape(count, TOK, HEAD_WIDTH)

        for count in range(1, MOST_BLOCKS + 1):
            pl.when(i - first_block + 1 == count)(lambda count=count: with_blocks(count))
        return carry

    lax.fori_loop(0, BLOCKS, query_block, 0)
    at = GROUP * TOK
    out_ref[:, at : at + TOK, :] = (dk_ref[...] * scale).astype(jnp.bfloat16)
    out_ref[:, at + TOK : at + 2 * TOK, :] = dv_ref[...].astype(jnp.bfloat16)


def unpack_kernel(back_ref, dq_ref, dk_ref, dv_ref):
    for h in range(GROUP):
        dq_ref[:, h * HEAD_WIDTH : (h + 1) * HEAD_WIDTH] = back_ref[0, h * TOK : (h + 1) * TOK, :]
    at = GROUP * TOK
    dk_ref[...] = back_ref[0, at : at + TOK, :]
    dv_ref[...] = back_ref[0, at + TOK : at + 2 * TOK, :]


def local(queries, keys, values, outputs, output_gradient, doc_ids):
    wide = pl.BlockSpec((TOK, GROUP * HEAD_WIDTH), lambda g: (0, g))
    narrow = pl.BlockSpec((TOK, HEAD_WIDTH), lambda g: (0, g))
    docs = jnp.tile(doc_ids, 2).reshape(3, 128).astype(jnp.float32)
    packed = pl.pallas_call(
        pack_kernel,
        grid=(KEY_VALUE_HEADS,),
        in_specs=[wide, narrow, narrow, wide, wide, pl.BlockSpec((3, 128), lambda g: (0, 0))],
        out_specs=pl.BlockSpec((1, SEND_ROWS, 128), lambda g: (g, 0, 0)),
        out_shape=jax.ShapeDtypeStruct((KEY_VALUE_HEADS, SEND_ROWS, 128), jnp.bfloat16),
        compiler_params=pltpu.CompilerParams(vmem_limit_bytes=32 * 2**20),
        name="pack",
    )(queries, keys, values, outputs, output_gradient, docs)
    payload = lax.all_to_all(packed, "blk", 0, 0, tiled=True)
    result = pl.pallas_call(
        attention_kernel,
        out_shape=jax.ShapeDtypeStruct((BLOCKS, BACK_ROWS, 128), jnp.bfloat16),
        scratch_shapes=[
            pltpu.VMEM((BLOCKS, 16, 128), jnp.float32),
            pltpu.VMEM((BLOCKS, 8, 128), jnp.float32),
            pltpu.SMEM((BLOCKS,), jnp.int32),
            pltpu.VMEM((BLOCKS, TOK, HEAD_WIDTH), jnp.float32),
            pltpu.VMEM((BLOCKS, TOK, HEAD_WIDTH), jnp.float32),
        ],
        compiler_params=pltpu.CompilerParams(vmem_limit_bytes=48 * 2**20),
        name="attention",
    )(payload)
    back = lax.all_to_all(result, "blk", 0, 0, tiled=True)
    return pl.pallas_call(
        unpack_kernel,
        grid=(KEY_VALUE_HEADS,),
        in_specs=[pl.BlockSpec((1, BACK_ROWS, 128), lambda g: (g, 0, 0))],
        out_specs=[wide, narrow, narrow],
        out_shape=[
            jax.ShapeDtypeStruct(queries.shape, jnp.bfloat16),
            jax.ShapeDtypeStruct(keys.shape, jnp.bfloat16),
            jax.ShapeDtypeStruct(values.shape, jnp.bfloat16),
        ],
        compiler_params=pltpu.CompilerParams(vmem_limit_bytes=32 * 2**20),
        name="unpack",
    )(back)


def solution(mesh):
    rows = P(("dp", "blk"), None)
    return jax.shard_map(
        local,
        mesh=mesh,
        in_specs=(rows, rows, rows, rows, rows, P(("dp", "blk"))),
        out_specs=(rows, rows, rows),
        check_vma=False,
    )
```

```python
import math

import jax
import jax.numpy as jnp
from jax import lax
from jax.experimental import pallas as pl
from jax.experimental.pallas import tpu as pltpu
from jax.sharding import PartitionSpec as P

QUERY_HEADS = 32
KEY_VALUE_HEADS = 8
HEAD_WIDTH = 128
GROUP = QUERY_HEADS // KEY_VALUE_HEADS
DOCS = 8
TOK = 192
BLOCKS = 8
MOST_BLOCKS = 5
WIDE = GROUP * TOK
Q_AT = 0
G_AT = GROUP * TOK
K_AT = 2 * GROUP * TOK
V_AT = K_AT + TOK
X_AT = V_AT + TOK
SEND_ROWS = X_AT + 16
BACK_ROWS = (GROUP + 2) * TOK
NT = (((1,), (1,)), ((), ()))
TN = (((0,), (0,)), ((), ()))
NN = (((1,), (0,)), ((), ()))


def dot(a, b, dims):
    return lax.dot_general(a, b, dims, preferred_element_type=jnp.float32)


def pack_kernel(q_ref, k_ref, v_ref, o_ref, g_ref, doc_ref, out_ref, send, o_buf, g_sem, kv_sem, sem):
    def column(ref, at):
        return ref.at[:, at * HEAD_WIDTH : (at + 1) * HEAD_WIDTH]

    arrivals = []
    for group in range(KEY_VALUE_HEADS):
        copies = []
        for h in range(GROUP):
            head = group * GROUP + h
            rows = pl.ds(G_AT + h * TOK, TOK)
            own = pl.ds(h * TOK, TOK)
            copies += [
                pltpu.make_async_copy(column(g_ref, head), send.at[group, rows], g_sem.at[0, head]),
                pltpu.make_async_copy(column(o_ref, head), o_buf.at[group, own], g_sem.at[1, head]),
                pltpu.make_async_copy(column(q_ref, head), send.at[group, own], g_sem.at[2, head]),
            ]
        for n, (ref, at) in enumerate(((k_ref, K_AT), (v_ref, V_AT))):
            rows = pl.ds(at, TOK)
            copies.append(
                pltpu.make_async_copy(column(ref, group), send.at[group, rows], kv_sem.at[n, group])
            )
        for copy in copies:
            copy.start()
        arrivals.append(copies)
    doc = doc_ref[...].astype(jnp.float32)
    doc = jnp.concatenate([doc, doc], axis=1)
    tail = jnp.concatenate([doc[:, t * 128 : (t + 1) * 128] for t in range(3)], axis=0)
    tail = jnp.concatenate([tail, jnp.zeros((1, 128), jnp.float32)], axis=0)
    departures = []
    for group in range(KEY_VALUE_HEADS):
        for copy in arrivals[group]:
            copy.wait()
        g = send[group, G_AT : G_AT + WIDE, :].astype(jnp.float32)
        product = g * o_buf[group].astype(jnp.float32)
        delta = jnp.sum(product.T, axis=0, keepdims=True)
        delta = jnp.concatenate([delta[:, t * 128 : (t + 1) * 128] for t in range(6)], axis=0)
        high = delta.astype(jnp.bfloat16).astype(jnp.float32)
        extra = jnp.concatenate([high, delta - high, tail], axis=0)
        send[group, X_AT : X_AT + 16, :] = extra.astype(jnp.bfloat16)
        departures.append(pltpu.make_async_copy(send.at[group], out_ref.at[group], sem.at[group]))
        departures[group].start()
    for copy in departures:
        copy.wait()


def attention_kernel(pay_ref, out_ref, extra_ref, start_ref, first_ref, dk_ref, dv_ref):
    scale = 1.0 / math.sqrt(HEAD_WIDTH)
    to_exp2 = scale * math.log2(math.e)
    dk_ref[...] = jnp.zeros_like(dk_ref)
    dv_ref[...] = jnp.zeros_like(dv_ref)
    for b in range(BLOCKS):
        extra_ref[b] = pay_ref[b, X_AT : X_AT + 16, :].astype(jnp.float32)
    docs = jnp.concatenate([extra_ref[b, 12:15, :] for b in range(BLOCKS)], axis=0)
    starts = jnp.zeros_like(docs)
    for d in range(1, DOCS):
        before = 0.5 * jnp.sum(jnp.where(docs < d, 1.0, 0.0), keepdims=True)
        starts = jnp.where(docs == d, before, starts)
    for b in range(BLOCKS):
        own = starts[3 * b : 3 * b + 3]
        start_ref[b] = jnp.concatenate([own, own, own[:2]], axis=0)
        first_ref[b] = jnp.min(own).astype(jnp.int32)

    def query_block(i, carry):
        first_block = first_ref[i] // TOK
        first_row = start_ref[i]
        start = jnp.concatenate([first_row[t : t + 1] for t in range(6)], axis=1).astype(jnp.int32)
        delta6 = extra_ref[i, 0:6, :] + extra_ref[i, 6:12, :]
        delta = jnp.concatenate([delta6[t : t + 1] for t in range(6)], axis=1)
        lane = lax.broadcasted_iota(jnp.int32, (1, WIDE), 1)
        own_row = lane
        for h in range(1, GROUP):
            own_row = jnp.where(lane >= h * TOK, lane - h * TOK, own_row)

        def with_blocks(count):
            low = i - count + 1
            rows = count * TOK
            keys = pay_ref[pl.ds(low, count), K_AT : K_AT + TOK, :].reshape(rows, HEAD_WIDTH)
            values = pay_ref[pl.ds(low, count), V_AT : V_AT + TOK, :].reshape(rows, HEAD_WIDTH)
            q = pay_ref[i, Q_AT : Q_AT + WIDE, :]
            g = pay_ref[i, G_AT : G_AT + WIDE, :]
            key_row = lax.broadcasted_iota(jnp.int32, (rows, WIDE), 0)
            scores = jnp.where(key_row >= start - low * TOK, dot(keys, q, NT), -1e30)
            edge = jnp.where(key_row[:TOK] <= own_row, scores[rows - TOK :], -1e30)
            scores = jnp.concatenate([scores[: rows - TOK], edge], axis=0) if count > 1 else edge
            top = jnp.max(scores, axis=0, keepdims=True)
            weights = jnp.exp2(scores * to_exp2 - top * to_exp2)
            total = jnp.sum(weights, axis=0, keepdims=True)
            probs = weights * (1.0 / total)
            dv = dot(probs.astype(jnp.bfloat16), g, NN)
            prob_grad = dot(values, g, NT)
            score_grad = (probs * (prob_grad - delta)).astype(jnp.bfloat16)
            dk = dot(score_grad, q, NN)
            dq = dot(keys, score_grad, TN).T
            out_ref[i, 0:WIDE, :] = (dq * scale).astype(jnp.bfloat16)
            dk_ref[pl.ds(low, count)] += dk.reshape(count, TOK, HEAD_WIDTH)
            dv_ref[pl.ds(low, count)] += dv.reshape(count, TOK, HEAD_WIDTH)

        for count in range(1, MOST_BLOCKS + 1):
            pl.when(i - first_block + 1 == count)(lambda count=count: with_blocks(count))
        return carry

    lax.fori_loop(0, BLOCKS, query_block, 0)
    at = GROUP * TOK
    out_ref[:, at : at + TOK, :] = (dk_ref[...] * scale).astype(jnp.bfloat16)
    out_ref[:, at + TOK : at + 2 * TOK, :] = dv_ref[...].astype(jnp.bfloat16)


def unpack_kernel(back_ref, dq_ref, dk_ref, dv_ref, sem):
    copies = []

    def send(group, at, ref, column):
        copies.append(
            pltpu.make_async_copy(
                back_ref.at[group, pl.ds(at, TOK)],
                ref.at[:, column * HEAD_WIDTH : (column + 1) * HEAD_WIDTH],
                sem.at[len(copies)],
            )
        )

    for group in range(KEY_VALUE_HEADS):
        for h in range(GROUP):
            send(group, h * TOK, dq_ref, group * GROUP + h)
        send(group, GROUP * TOK, dk_ref, group)
        send(group, (GROUP + 1) * TOK, dv_ref, group)
    for copy in copies:
        copy.start()
    for copy in copies:
        copy.wait()


def local(queries, keys, values, outputs, output_gradient, doc_ids):
    hbm = pl.BlockSpec(memory_space=pltpu.HBM)
    vmem = pl.BlockSpec(memory_space=pltpu.VMEM)
    packed = pl.pallas_call(
        pack_kernel,
        in_specs=[hbm] * 5 + [vmem],
        out_specs=hbm,
        out_shape=jax.ShapeDtypeStruct((KEY_VALUE_HEADS, SEND_ROWS, 128), jnp.bfloat16),
        scratch_shapes=[
            pltpu.VMEM((KEY_VALUE_HEADS, SEND_ROWS, 128), jnp.bfloat16),
            pltpu.VMEM((KEY_VALUE_HEADS, WIDE, HEAD_WIDTH), jnp.bfloat16),
            pltpu.SemaphoreType.DMA((3, QUERY_HEADS)),
            pltpu.SemaphoreType.DMA((2, KEY_VALUE_HEADS)),
            pltpu.SemaphoreType.DMA((KEY_VALUE_HEADS,)),
        ],
        compiler_params=pltpu.CompilerParams(vmem_limit_bytes=62 * 2**20),
        name="pack",
    )(queries, keys, values, outputs, output_gradient, doc_ids.reshape(1, TOK))
    payload = lax.all_to_all(packed, "blk", 0, 0, tiled=True)
    result = pl.pallas_call(
        attention_kernel,
        out_shape=jax.ShapeDtypeStruct((BLOCKS, BACK_ROWS, 128), jnp.bfloat16),
        scratch_shapes=[
            pltpu.VMEM((BLOCKS, 16, 128), jnp.float32),
            pltpu.VMEM((BLOCKS, 8, 128), jnp.float32),
            pltpu.SMEM((BLOCKS,), jnp.int32),
            pltpu.VMEM((BLOCKS, TOK, HEAD_WIDTH), jnp.float32),
            pltpu.VMEM((BLOCKS, TOK, HEAD_WIDTH), jnp.float32),
        ],
        compiler_params=pltpu.CompilerParams(vmem_limit_bytes=32 * 2**20),
        name="attention",
    )(payload)
    back = lax.all_to_all(result, "blk", 0, 0, tiled=True)
    return pl.pallas_call(
        unpack_kernel,
        in_specs=[pl.BlockSpec(memory_space=pl.ANY)],
        out_specs=[hbm] * 3,
        out_shape=[
            jax.ShapeDtypeStruct(queries.shape, jnp.bfloat16),
            jax.ShapeDtypeStruct(keys.shape, jnp.bfloat16),
            jax.ShapeDtypeStruct(values.shape, jnp.bfloat16),
        ],
        scratch_shapes=[pltpu.SemaphoreType.DMA((QUERY_HEADS + 2 * KEY_VALUE_HEADS,))],
        compiler_params=pltpu.CompilerParams(vmem_limit_bytes=32 * 2**20),
        name="unpack",
    )(back)


def solution(mesh):
    rows = P(("dp", "blk"), None)
    return jax.shard_map(
        local,
        mesh=mesh,
        in_specs=(rows, rows, rows, rows, rows, P(("dp", "blk"))),
        out_specs=(rows, rows, rows),
        check_vma=False,
    )
```

```python
import functools
import math

import jax
import jax.numpy as jnp
from jax import lax
from jax.experimental import pallas as pl
from jax.experimental.pallas import tpu as pltpu
from jax.sharding import PartitionSpec as P

QUERY_HEADS = 32
KEY_VALUE_HEADS = 8
HEAD_WIDTH = 128
GROUP = QUERY_HEADS // KEY_VALUE_HEADS
DOCS = 8
TOK = 192
BLOCKS = 8
MOST_BLOCKS = 5
UNIT = 64
UNITS = TOK // UNIT
LANES = GROUP * UNIT
Q_AT = 0
G_AT = GROUP * TOK
K_AT = 2 * GROUP * TOK
V_AT = K_AT + TOK
X_AT = V_AT + TOK
SEND_ROWS = X_AT + 16
BACK_ROWS = (GROUP + 2) * TOK
NT = (((1,), (1,)), ((), ()))
TN = (((0,), (0,)), ((), ()))
NN = (((1,), (0,)), ((), ()))


def dot(a, b, dims):
    return lax.dot_general(a, b, dims, preferred_element_type=jnp.float32)


def pack_kernel(
    q_ref, k_ref, v_ref, o_ref, g_ref, doc_ref, out_ref, q_buf, k_buf, v_buf, o_buf, g_buf, doc_buf, send, in_sem, kv_sem, sem
):
    whole = [
        pltpu.make_async_copy(k_ref, k_buf, kv_sem.at[0]),
        pltpu.make_async_copy(v_ref, v_buf, kv_sem.at[1]),
        pltpu.make_async_copy(doc_ref, doc_buf, kv_sem.at[2]),
    ]
    arrivals = []
    for group in range(KEY_VALUE_HEADS):
        cols = slice(group * GROUP * HEAD_WIDTH, (group + 1) * GROUP * HEAD_WIDTH)
        arrivals.append(
            [
                pltpu.make_async_copy(ref.at[:, cols], buf.at[:, cols], in_sem.at[n, group])
                for n, (ref, buf) in enumerate(((g_ref, g_buf), (o_ref, o_buf), (q_ref, q_buf)))
            ]
        )
        for copy in arrivals[group]:
            copy.start()
        if group == 0:
            for copy in whole:
                copy.start()
    departures = []
    for group in range(KEY_VALUE_HEADS):
        for copy in arrivals[group]:
            copy.wait()
        if group == 0:
            for copy in whole:
                copy.wait()
            doc = doc_buf[...].astype(jnp.float32)
            tail = [doc[:, t * UNIT : (t + 1) * UNIT] for t in range(UNITS)]
            tail = [jnp.concatenate([part, part], axis=1) for part in tail]
            tail = jnp.concatenate(tail + [jnp.zeros((1, 128), jnp.float32)], axis=0)
        product = []
        for t in range(UNITS):
            rows = slice(t * UNIT, (t + 1) * UNIT)
            for h in range(GROUP):
                head = group * GROUP + h
                cols = slice(head * HEAD_WIDTH, (head + 1) * HEAD_WIDTH)
                at = t * LANES + h * UNIT
                g = g_buf[rows, cols]
                send[group, Q_AT + at : Q_AT + at + UNIT, :] = q_buf[rows, cols]
                send[group, G_AT + at : G_AT + at + UNIT, :] = g
                product.append(g.astype(jnp.float32) * o_buf[rows, cols].astype(jnp.float32))
        own = slice(group * HEAD_WIDTH, (group + 1) * HEAD_WIDTH)
        send[group, K_AT : K_AT + TOK, :] = k_buf[:, own]
        send[group, V_AT : V_AT + TOK, :] = v_buf[:, own]
        delta = jnp.sum(jnp.concatenate(product, axis=0).T, axis=0, keepdims=True)
        delta = jnp.concatenate([delta[:, t * 128 : (t + 1) * 128] for t in range(6)], axis=0)
        high = delta.astype(jnp.bfloat16).astype(jnp.float32)
        extra = jnp.concatenate([high, delta - high, tail], axis=0)
        send[group, X_AT : X_AT + 16, :] = extra.astype(jnp.bfloat16)
        departures.append(pltpu.make_async_copy(send.at[group], out_ref.at[group], sem.at[group]))
        departures[group].start()
    for copy in departures:
        copy.wait()


def attention_kernel(pay_ref, out_ref, extra_ref, start_ref, first_ref, dk_ref, dv_ref):
    scale = 1.0 / math.sqrt(HEAD_WIDTH)
    to_exp2 = scale * math.log2(math.e)
    dk_ref[...] = jnp.zeros_like(dk_ref)
    dv_ref[...] = jnp.zeros_like(dv_ref)
    for b in range(BLOCKS):
        extra_ref[b] = pay_ref[b, X_AT : X_AT + 16, :].astype(jnp.float32)
    docs = jnp.concatenate([extra_ref[b, 12:15, :] for b in range(BLOCKS)], axis=0)
    starts = jnp.zeros_like(docs)
    for d in range(1, DOCS):
        before = 0.5 * jnp.sum(jnp.where(docs < d, 1.0, 0.0), keepdims=True)
        starts = jnp.where(docs == d, before, starts)
    for b in range(BLOCKS):
        own = starts[UNITS * b : UNITS * (b + 1)]
        start_ref[b] = jnp.concatenate([own, own, own[:2]], axis=0)
        first_ref[b] = jnp.min(own).astype(jnp.int32)

    def query_block(i, carry):
        first_block = first_ref[i] // TOK
        start3 = start_ref[i].astype(jnp.int32)
        delta6 = extra_ref[i, 0:6, :] + extra_ref[i, 6:12, :]

        def with_blocks(count):
            low = i - count + 1
            row0 = pl.multiple_of(low * TOK, TOK)
            keys = pay_ref[pl.ds(low, count), K_AT : K_AT + TOK, :].reshape(count * TOK, HEAD_WIDTH)
            values = pay_ref[pl.ds(low, count), V_AT : V_AT + TOK, :].reshape(
                count * TOK, HEAD_WIDTH
            )
            token = lax.broadcasted_iota(jnp.int32, (UNIT, LANES), 1) % UNIT
            causal = lax.broadcasted_iota(jnp.int32, (UNIT, LANES), 0) <= token

            def load(t, at):
                return pay_ref[i, at + t * LANES : at + (t + 1) * LANES, :]

            def rows_at(t, j):
                return TOK if j + 1 < count else (t + 1) * UNIT

            def scores_of(t, j):
                return dot(keys[j * TOK : j * TOK + rows_at(t, j)], load(t, Q_AT), NT)

            def weigh(t, j, scores):
                rows = rows_at(t, j)
                start = jnp.concatenate([start3[t : t + 1]] * 2, axis=1) - (low + j) * TOK
                key_row = lax.broadcasted_iota(jnp.int32, (rows, LANES), 0)
                scores = jnp.where(key_row >= start, scores, -1e30)
                if j + 1 == count:
                    edge = jnp.where(causal, scores[rows - UNIT :], -1e30)
                    scores = jnp.concatenate([scores[: rows - UNIT], edge], axis=0) if t else edge
                top = jnp.max(scores, axis=0, keepdims=True) * to_exp2
                weights = jnp.exp2(scores * to_exp2 - top)
                return weights, top, jnp.sum(weights, axis=0, keepdims=True)

            def factors(parts):
                top = functools.reduce(jnp.maximum, [part[1] for part in parts])
                shares = [jnp.exp2(part[1] - top) for part in parts]
                total = functools.reduce(
                    jnp.add, [share * part[2] for share, part in zip(shares, parts)]
                )
                inverse = 1.0 / total
                return [share * inverse for share in shares]

            def grads(t, j, weights, factor, prob_grad):
                delta = jnp.concatenate(
                    [delta6[2 * t : 2 * t + 1], delta6[2 * t + 1 : 2 * t + 2]], axis=1
                )
                probs = weights * factor
                return probs.astype(jnp.bfloat16), (probs * (prob_grad - delta)).astype(jnp.bfloat16)

            def prob_grad_of(t, j):
                return dot(values[j * TOK : j * TOK + rows_at(t, j)], load(t, G_AT), NT)

            def accumulate(t, j, probs, score_grad):
                rows = rows_at(t, j)
                at = pl.ds(pl.multiple_of(row0 + j * TOK, UNIT), rows)
                dv_ref[at] += dot(probs, load(t, G_AT), NN)
                dk_ref[at] += dot(score_grad, load(t, Q_AT), NN)

            def finish(t, score_grads):
                rows = (count - 1) * TOK + (t + 1) * UNIT
                score_grad = jnp.concatenate(score_grads, axis=0) if count > 1 else score_grads[0]
                dq = (dot(keys[:rows], score_grad, TN) * scale).T.astype(jnp.bfloat16)
                for h in range(GROUP):
                    at = h * TOK + t * UNIT
                    out_ref[i, at : at + UNIT, :] = dq[h * UNIT : (h + 1) * UNIT]

            blocks = range(count)
            parts = []
            for t in range(UNITS):
                ahead = scores_of(t, 0)
                parts.append([])
                for j in blocks:
                    now, ahead = ahead, scores_of(t, j + 1) if j + 1 < count else None
                    parts[t].append(weigh(t, j, now))
            factor = [factors(part) for part in parts]
            steps = [(t, j) for t in range(UNITS) for j in blocks]
            ahead = prob_grad_of(*steps[0])
            done = {}
            for n, step in enumerate(steps):
                t, j = step
                now, ahead = ahead, prob_grad_of(*steps[n + 1]) if n + 1 < len(steps) else None
                done[step] = grads(t, j, parts[t][j][0], factor[t][j], now)
                if n:
                    accumulate(*steps[n - 1], *done[steps[n - 1]])
                if j + 1 == count:
                    finish(t, [done[t, k][1] for k in blocks])
            accumulate(*steps[-1], *done[steps[-1]])

        for count in range(1, MOST_BLOCKS + 1):
            pl.when(i - first_block + 1 == count)(lambda count=count: with_blocks(count))
        return carry

    lax.fori_loop(0, BLOCKS, query_block, 0)
    at = GROUP * TOK
    for b in range(BLOCKS):
        own = slice(b * TOK, (b + 1) * TOK)
        out_ref[b, at : at + TOK, :] = (dk_ref[own] * scale).astype(jnp.bfloat16)
        out_ref[b, at + TOK : at + 2 * TOK, :] = dv_ref[own].astype(jnp.bfloat16)


def unpack_kernel(back_ref, dq_ref, dk_ref, dv_ref, sem):
    copies = []

    def send(group, at, ref, column):
        copies.append(
            pltpu.make_async_copy(
                back_ref.at[group, pl.ds(at, TOK)],
                ref.at[:, column * HEAD_WIDTH : (column + 1) * HEAD_WIDTH],
                sem.at[len(copies)],
            )
        )

    for group in range(KEY_VALUE_HEADS):
        for h in range(GROUP):
            send(group, h * TOK, dq_ref, group * GROUP + h)
        send(group, GROUP * TOK, dk_ref, group)
        send(group, (GROUP + 1) * TOK, dv_ref, group)
    for copy in copies:
        copy.start()
    for copy in copies:
        copy.wait()


def local(queries, keys, values, outputs, output_gradient, doc_ids):
    hbm = pl.BlockSpec(memory_space=pltpu.HBM)
    packed = pl.pallas_call(
        pack_kernel,
        in_specs=[hbm] * 6,
        out_specs=hbm,
        out_shape=jax.ShapeDtypeStruct((KEY_VALUE_HEADS, SEND_ROWS, 128), jnp.bfloat16),
        scratch_shapes=[
            pltpu.VMEM(queries.shape, jnp.bfloat16),
            pltpu.VMEM(keys.shape, jnp.bfloat16),
            pltpu.VMEM(values.shape, jnp.bfloat16),
            pltpu.VMEM(outputs.shape, jnp.bfloat16),
            pltpu.VMEM(output_gradient.shape, jnp.bfloat16),
            pltpu.VMEM((1, TOK), jnp.int32),
            pltpu.VMEM((KEY_VALUE_HEADS, SEND_ROWS, 128), jnp.bfloat16),
            pltpu.SemaphoreType.DMA((3, KEY_VALUE_HEADS)),
            pltpu.SemaphoreType.DMA((3,)),
            pltpu.SemaphoreType.DMA((KEY_VALUE_HEADS,)),
        ],
        compiler_params=pltpu.CompilerParams(vmem_limit_bytes=62 * 2**20),
        name="pack",
    )(queries, keys, values, outputs, output_gradient, doc_ids.reshape(1, TOK))
    payload = lax.all_to_all(packed, "blk", 0, 0, tiled=True)
    result = pl.pallas_call(
        attention_kernel,
        out_shape=jax.ShapeDtypeStruct((BLOCKS, BACK_ROWS, 128), jnp.bfloat16),
        scratch_shapes=[
            pltpu.VMEM((BLOCKS, 16, 128), jnp.float32),
            pltpu.VMEM((BLOCKS, 8, 128), jnp.float32),
            pltpu.SMEM((BLOCKS,), jnp.int32),
            pltpu.VMEM((BLOCKS * TOK, HEAD_WIDTH), jnp.float32),
            pltpu.VMEM((BLOCKS * TOK, HEAD_WIDTH), jnp.float32),
        ],
        compiler_params=pltpu.CompilerParams(vmem_limit_bytes=32 * 2**20),
        name="attention",
    )(payload)
    back = lax.all_to_all(result, "blk", 0, 0, tiled=True)
    return pl.pallas_call(
        unpack_kernel,
        in_specs=[pl.BlockSpec(memory_space=pl.ANY)],
        out_specs=[hbm] * 3,
        out_shape=[
            jax.ShapeDtypeStruct(queries.shape, jnp.bfloat16),
            jax.ShapeDtypeStruct(keys.shape, jnp.bfloat16),
            jax.ShapeDtypeStruct(values.shape, jnp.bfloat16),
        ],
        scratch_shapes=[pltpu.SemaphoreType.DMA((QUERY_HEADS + 2 * KEY_VALUE_HEADS,))],
        compiler_params=pltpu.CompilerParams(vmem_limit_bytes=32 * 2**20),
        name="unpack",
    )(back)


def solution(mesh):
    rows = P(("dp", "blk"), None)
    return jax.shard_map(
        local,
        mesh=mesh,
        in_specs=(rows, rows, rows, rows, rows, P(("dp", "blk"))),
        out_specs=(rows, rows, rows),
        check_vma=False,
    )
```

```python
import functools
import math

import jax
import jax.numpy as jnp
from jax import lax
from jax.experimental import pallas as pl
from jax.experimental.pallas import tpu as pltpu
from jax.sharding import PartitionSpec as P

QUERY_HEADS = 32
KEY_VALUE_HEADS = 8
HEAD_WIDTH = 128
GROUP = QUERY_HEADS // KEY_VALUE_HEADS
DOCS = 8
TOK = 192
BLOCKS = 8
MOST_BLOCKS = 5
UNIT = 64
UNITS = TOK // UNIT
LANES = GROUP * UNIT
KINDS = MOST_BLOCKS + 1
TOGETHER = [(n, n + 1) for n in range(1, MOST_BLOCKS)] + [(n, 0) for n in range(KINDS)]
SHORT = 3 * UNIT
Q_AT = 0
G_AT = GROUP * TOK
K_AT = 2 * GROUP * TOK
V_AT = K_AT + TOK
X_AT = V_AT + TOK
SEND_ROWS = X_AT + 16
BACK_ROWS = (GROUP + 2) * TOK
NT = (((1,), (1,)), ((), ()))
TN = (((0,), (0,)), ((), ()))
NN = (((1,), (0,)), ((), ()))


def dot(a, b, dims):
    return lax.dot_general(a, b, dims, preferred_element_type=jnp.float32)


def pack_kernel(
    q_ref, k_ref, v_ref, o_ref, g_ref, doc_ref, out_ref, q_buf, k_buf, v_buf, o_buf, g_buf, doc_buf, send, in_sem, kv_sem, sem
):
    whole = [
        pltpu.make_async_copy(k_ref, k_buf, kv_sem.at[0]),
        pltpu.make_async_copy(v_ref, v_buf, kv_sem.at[1]),
        pltpu.make_async_copy(doc_ref, doc_buf, kv_sem.at[2]),
    ]
    arrivals = []
    for group in range(KEY_VALUE_HEADS):
        cols = slice(group * GROUP * HEAD_WIDTH, (group + 1) * GROUP * HEAD_WIDTH)
        arrivals.append(
            [
                pltpu.make_async_copy(ref.at[:, cols], buf.at[:, cols], in_sem.at[n, group])
                for n, (ref, buf) in enumerate(((g_ref, g_buf), (o_ref, o_buf), (q_ref, q_buf)))
            ]
        )
        for copy in arrivals[group]:
            copy.start()
        if group == 0:
            for copy in whole:
                copy.start()
    departures = []
    for group in range(KEY_VALUE_HEADS):
        for copy in arrivals[group]:
            copy.wait()
        if group == 0:
            for copy in whole:
                copy.wait()
            doc = doc_buf[...].astype(jnp.float32)
            tail = [doc[:, t * UNIT : (t + 1) * UNIT] for t in range(UNITS)]
            tail = [jnp.concatenate([part, part], axis=1) for part in tail]
            tail = jnp.concatenate(tail + [jnp.zeros((1, 128), jnp.float32)], axis=0)
        product = []
        for t in range(UNITS):
            rows = slice(t * UNIT, (t + 1) * UNIT)
            for h in range(GROUP):
                head = group * GROUP + h
                cols = slice(head * HEAD_WIDTH, (head + 1) * HEAD_WIDTH)
                at = t * LANES + h * UNIT
                g = g_buf[rows, cols]
                send[group, Q_AT + at : Q_AT + at + UNIT, :] = q_buf[rows, cols]
                send[group, G_AT + at : G_AT + at + UNIT, :] = g
                product.append(g.astype(jnp.float32) * o_buf[rows, cols].astype(jnp.float32))
        own = slice(group * HEAD_WIDTH, (group + 1) * HEAD_WIDTH)
        send[group, K_AT : K_AT + TOK, :] = k_buf[:, own]
        send[group, V_AT : V_AT + TOK, :] = v_buf[:, own]
        delta = jnp.sum(jnp.concatenate(product, axis=0).T, axis=0, keepdims=True)
        delta = jnp.concatenate([delta[:, t * 128 : (t + 1) * 128] for t in range(6)], axis=0)
        high = delta.astype(jnp.bfloat16).astype(jnp.float32)
        extra = jnp.concatenate([high, delta - high, tail], axis=0)
        send[group, X_AT : X_AT + 16, :] = extra.astype(jnp.bfloat16)
        departures.append(pltpu.make_async_copy(send.at[group], out_ref.at[group], sem.at[group]))
        departures[group].start()
    for copy in departures:
        copy.wait()


def attention_kernel(
    pay_ref, out_ref, extra_ref, start_ref, first_ref, reach_ref, dk_ref, dv_ref
):
    scale = 1.0 / math.sqrt(HEAD_WIDTH)
    to_exp2 = scale * math.log2(math.e)
    dk_ref[...] = jnp.zeros_like(dk_ref)
    dv_ref[...] = jnp.zeros_like(dv_ref)
    for b in range(BLOCKS):
        extra_ref[b] = pay_ref[b, X_AT : X_AT + 16, :].astype(jnp.float32)
    docs = jnp.concatenate([extra_ref[b, 12:15, :] for b in range(BLOCKS)], axis=0)
    starts = jnp.zeros_like(docs)
    for d in range(1, DOCS):
        before = 0.5 * jnp.sum(jnp.where(docs < d, 1.0, 0.0), keepdims=True)
        starts = jnp.where(docs == d, before, starts)
    for b in range(BLOCKS):
        own = starts[UNITS * b : UNITS * (b + 1)]
        start_ref[b] = jnp.concatenate([own, own, own[:2]], axis=0)
        first_ref[b] = jnp.min(own).astype(jnp.int32)
        chunk_at = b * TOK + UNIT * lax.broadcasted_iota(jnp.int32, own.shape, 0)
        reach_ref[b] = jnp.max(chunk_at.astype(jnp.float32) - own).astype(jnp.int32)

    def kind_of(i):
        first_block = first_ref[i] // TOK
        is_short = (i > 0) & (reach_ref[i] <= SHORT - UNIT) & (first_block < i)
        return jnp.where(is_short, 0, i - first_block + 1)

    def chunks_of(i, kind):
        short = kind == 0
        count = kind or 2
        start3 = start_ref[i].astype(jnp.int32)
        delta6 = extra_ref[i, 0:6, :] + extra_ref[i, 6:12, :]
        low = i - count + 1
        row0 = pl.multiple_of(low * TOK, TOK)
        keys = pay_ref[pl.ds(low, count), K_AT : K_AT + TOK, :].reshape(count * TOK, HEAD_WIDTH)
        values = pay_ref[pl.ds(low, count), V_AT : V_AT + TOK, :].reshape(
            count * TOK, HEAD_WIDTH
        )
        token = lax.broadcasted_iota(jnp.int32, (UNIT, LANES), 1) % UNIT
        causal = lax.broadcasted_iota(jnp.int32, (UNIT, LANES), 0) <= token

        def load(t, at):
            return pay_ref[i, at + t * LANES : at + (t + 1) * LANES, :]

        def end(t):
            return (count - 1) * TOK + (t + 1) * UNIT

        def begin(t):
            return end(t) - SHORT if short else 0

        def pieces(t):
            edges = list(range(begin(t), end(t), TOK)) + [end(t)]
            return [slice(p - begin(t), q - begin(t)) for p, q in zip(edges, edges[1:])]

        def scores_of(t):
            return dot(keys[begin(t) : end(t)], load(t, Q_AT), NT)

        def prob_grad_of(t):
            return dot(values[begin(t) : end(t)], load(t, G_AT), NT)

        def weigh(t, scores):
            start = jnp.concatenate([start3[t : t + 1]] * 2, axis=1) - (low * TOK + begin(t))
            parts = []
            for piece in pieces(t):
                rows = piece.stop - piece.start
                key_row = lax.broadcasted_iota(jnp.int32, (rows, LANES), 0)
                part = jnp.where(key_row >= start - piece.start, scores[piece], -1e30)
                if piece.stop == end(t) - begin(t):
                    edge = jnp.where(causal, part[rows - UNIT :], -1e30)
                    part = jnp.concatenate([part[: rows - UNIT], edge], axis=0) if rows > UNIT else edge
                top = jnp.max(part, axis=0, keepdims=True) * to_exp2
                weights = jnp.exp2(part * to_exp2 - top)
                parts.append((weights, top, jnp.sum(weights, axis=0, keepdims=True)))
            return parts

        def factors(parts):
            top = functools.reduce(jnp.maximum, [part[1] for part in parts])
            shares = [jnp.exp2(part[1] - top) for part in parts]
            total = functools.reduce(
                jnp.add, [share * part[2] for share, part in zip(shares, parts)]
            )
            inverse = 1.0 / total
            return [share * inverse for share in shares]

        def grads(t, parts, prob_grad):
            delta = jnp.concatenate(
                [delta6[2 * t : 2 * t + 1], delta6[2 * t + 1 : 2 * t + 2]], axis=1
            )
            low_probs, score_grads = [], []
            for piece, part, factor in zip(pieces(t), parts, factors(parts)):
                probs = part[0] * factor
                low_probs.append(probs.astype(jnp.bfloat16))
                score_grads.append((probs * (prob_grad[piece] - delta)).astype(jnp.bfloat16))
            if len(parts) == 1:
                return low_probs[0], score_grads[0]
            return jnp.concatenate(low_probs, axis=0), jnp.concatenate(score_grads, axis=0)

        def finish(t, probs, score_grad):
            at = pl.ds(pl.multiple_of(row0 + begin(t), UNIT), end(t) - begin(t))
            dv_ref[at] += dot(probs, load(t, G_AT), NN)
            dk_ref[at] += dot(score_grad, load(t, Q_AT), NN)
            dq = dot(keys[begin(t) : end(t)], score_grad, TN) * scale
            dq = dq.T.astype(jnp.bfloat16)
            for h in range(GROUP):
                at = h * TOK + t * UNIT
                out_ref[i, at : at + UNIT, :] = dq[h * UNIT : (h + 1) * UNIT]

        def chunk(t):
            return tuple(
                functools.partial(step, t)
                for step in (scores_of, prob_grad_of, weigh, grads, finish)
            )

        return [chunk(t) for t in range(UNITS)]

    def run(chunks):
        count = len(chunks)
        s, d, w, g = {}, {}, {}, {}

        def scores_of(n):
            s[n] = chunks[n][0]()

        def grads(n):
            g[n] = chunks[n][3](w.pop(n), d.pop(n))

        scores_of(0)
        scores_of(1)
        for n in range(count):
            w[n] = chunks[n][2](s.pop(n))
            if n + 2 < count:
                scores_of(n + 2)
            d[n] = chunks[n][1]()
            if n > 1:
                chunks[n - 2][4](*g.pop(n - 2))
            if n > 0:
                grads(n - 1)
        chunks[-2][4](*g.pop(count - 2))
        grads(count - 1)
        chunks[-1][4](*g.pop(count - 1))

    def two_blocks(p, carry):
        first, second = kind_of(2 * p), kind_of(2 * p + 1)
        code = first * KINDS + second
        alone = code >= 0
        for one, two in TOGETHER:
            match = code == one * KINDS + two
            alone = alone & jnp.logical_not(match)
            pl.when(match)(
                lambda one=one, two=two: run(chunks_of(2 * p, one) + chunks_of(2 * p + 1, two))
            )

        @pl.when(alone)
        def _():
            def one_block(i, carry):
                kind = kind_of(i)
                for value in range(KINDS):
                    pl.when(kind == value)(lambda value=value: run(chunks_of(i, value)))
                return carry

            lax.fori_loop(2 * p, 2 * p + 2, one_block, 0)

        return carry

    lax.fori_loop(0, BLOCKS // 2, two_blocks, 0)
    at = GROUP * TOK
    for b in range(BLOCKS):
        own = slice(b * TOK, (b + 1) * TOK)
        out_ref[b, at : at + TOK, :] = (dk_ref[own] * scale).astype(jnp.bfloat16)
        out_ref[b, at + TOK : at + 2 * TOK, :] = dv_ref[own].astype(jnp.bfloat16)


def unpack_kernel(back_ref, dq_ref, dk_ref, dv_ref, sem):
    copies = []

    def send(group, at, ref, column):
        copies.append(
            pltpu.make_async_copy(
                back_ref.at[group, pl.ds(at, TOK)],
                ref.at[:, column * HEAD_WIDTH : (column + 1) * HEAD_WIDTH],
                sem.at[len(copies)],
            )
        )

    for group in range(KEY_VALUE_HEADS):
        for h in range(GROUP):
            send(group, h * TOK, dq_ref, group * GROUP + h)
        send(group, GROUP * TOK, dk_ref, group)
        send(group, (GROUP + 1) * TOK, dv_ref, group)
    for copy in copies:
        copy.start()
    for copy in copies:
        copy.wait()


def local(queries, keys, values, outputs, output_gradient, doc_ids):
    hbm = pl.BlockSpec(memory_space=pltpu.HBM)
    packed = pl.pallas_call(
        pack_kernel,
        in_specs=[hbm] * 6,
        out_specs=hbm,
        out_shape=jax.ShapeDtypeStruct((KEY_VALUE_HEADS, SEND_ROWS, 128), jnp.bfloat16),
        scratch_shapes=[
            pltpu.VMEM(queries.shape, jnp.bfloat16),
            pltpu.VMEM(keys.shape, jnp.bfloat16),
            pltpu.VMEM(values.shape, jnp.bfloat16),
            pltpu.VMEM(outputs.shape, jnp.bfloat16),
            pltpu.VMEM(output_gradient.shape, jnp.bfloat16),
            pltpu.VMEM((1, TOK), jnp.int32),
            pltpu.VMEM((KEY_VALUE_HEADS, SEND_ROWS, 128), jnp.bfloat16),
            pltpu.SemaphoreType.DMA((3, KEY_VALUE_HEADS)),
            pltpu.SemaphoreType.DMA((3,)),
            pltpu.SemaphoreType.DMA((KEY_VALUE_HEADS,)),
        ],
        compiler_params=pltpu.CompilerParams(vmem_limit_bytes=62 * 2**20),
        name="pack",
    )(queries, keys, values, outputs, output_gradient, doc_ids.reshape(1, TOK))
    payload = lax.all_to_all(packed, "blk", 0, 0, tiled=True)
    result = pl.pallas_call(
        attention_kernel,
        out_shape=jax.ShapeDtypeStruct((BLOCKS, BACK_ROWS, 128), jnp.bfloat16),
        scratch_shapes=[
            pltpu.VMEM((BLOCKS, 16, 128), jnp.float32),
            pltpu.VMEM((BLOCKS, 8, 128), jnp.float32),
            pltpu.SMEM((BLOCKS,), jnp.int32),
            pltpu.SMEM((BLOCKS,), jnp.int32),
            pltpu.VMEM((BLOCKS * TOK, HEAD_WIDTH), jnp.float32),
            pltpu.VMEM((BLOCKS * TOK, HEAD_WIDTH), jnp.float32),
        ],
        compiler_params=pltpu.CompilerParams(vmem_limit_bytes=32 * 2**20),
        name="attention",
    )(payload)
    back = lax.all_to_all(result, "blk", 0, 0, tiled=True)
    return pl.pallas_call(
        unpack_kernel,
        in_specs=[pl.BlockSpec(memory_space=pl.ANY)],
        out_specs=[hbm] * 3,
        out_shape=[
            jax.ShapeDtypeStruct(queries.shape, jnp.bfloat16),
            jax.ShapeDtypeStruct(keys.shape, jnp.bfloat16),
            jax.ShapeDtypeStruct(values.shape, jnp.bfloat16),
        ],
        scratch_shapes=[pltpu.SemaphoreType.DMA((QUERY_HEADS + 2 * KEY_VALUE_HEADS,))],
        compiler_params=pltpu.CompilerParams(vmem_limit_bytes=32 * 2**20),
        name="unpack",
    )(back)


def solution(mesh):
    rows = P(("dp", "blk"), None)
    return jax.shard_map(
        local,
        mesh=mesh,
        in_specs=(rows, rows, rows, rows, rows, P(("dp", "blk"))),
        out_specs=(rows, rows, rows),
        check_vma=False,
    )
```

```python
import functools
import math

import jax
import jax.numpy as jnp
from jax import lax
from jax.experimental import pallas as pl
from jax.experimental.pallas import tpu as pltpu
from jax.sharding import PartitionSpec as P

QUERY_HEADS = 32
KEY_VALUE_HEADS = 8
HEAD_WIDTH = 128
GROUP = QUERY_HEADS // KEY_VALUE_HEADS
DOCS = 8
TOK = 192
BLOCKS = 8
MOST_BLOCKS = 5
UNIT = 64
UNITS = TOK // UNIT
LANES = GROUP * UNIT
UNPACK_PARTS = 4
SHORT = 3 * UNIT
Q_AT = 0
G_AT = GROUP * TOK
K_AT = 2 * GROUP * TOK
V_AT = K_AT + TOK
X_AT = V_AT + TOK
SEND_ROWS = X_AT + 16
BACK_ROWS = (GROUP + 2) * TOK
NT = (((1,), (1,)), ((), ()))
TN = (((0,), (0,)), ((), ()))
NN = (((1,), (0,)), ((), ()))


def dot(a, b, dims):
    return lax.dot_general(a, b, dims, preferred_element_type=jnp.float32)


def pack_kernel(
    q_ref, k_ref, v_ref, o_ref, g_ref, doc_ref, out_ref, q_buf, k_buf, v_buf, o_buf, g_buf, doc_buf, send, extras, in_sem, kv_sem, sem, extra_sem
):
    whole = [
        pltpu.make_async_copy(k_ref, k_buf, kv_sem.at[0]),
        pltpu.make_async_copy(v_ref, v_buf, kv_sem.at[1]),
        pltpu.make_async_copy(doc_ref, doc_buf, kv_sem.at[2]),
    ]
    arrivals = []
    for group in range(KEY_VALUE_HEADS):
        cols = slice(group * GROUP * HEAD_WIDTH, (group + 1) * GROUP * HEAD_WIDTH)
        arrivals.append(
            [
                pltpu.make_async_copy(ref.at[:, cols], buf.at[:, cols], in_sem.at[n, group])
                for n, (ref, buf) in enumerate(((g_ref, g_buf), (o_ref, o_buf), (q_ref, q_buf)))
            ]
        )
        for copy in arrivals[group]:
            copy.start()
        if group == 0:
            for copy in whole:
                copy.start()
    departures = []
    for group in range(KEY_VALUE_HEADS):
        for copy in arrivals[group]:
            copy.wait()
        if group == 0:
            for copy in whole:
                copy.wait()
            doc = doc_buf[...].astype(jnp.float32)
            tail = [doc[:, t * UNIT : (t + 1) * UNIT] for t in range(UNITS)]
            tail = [jnp.concatenate([part, part], axis=1) for part in tail]
            tail = jnp.concatenate(tail + [jnp.zeros((1, 128), jnp.float32)], axis=0)
        product = []
        for t in range(UNITS):
            rows = slice(t * UNIT, (t + 1) * UNIT)
            for h in range(GROUP):
                head = group * GROUP + h
                cols = slice(head * HEAD_WIDTH, (head + 1) * HEAD_WIDTH)
                at = t * LANES + h * UNIT
                g = g_buf[rows, cols]
                send[group, Q_AT + at : Q_AT + at + UNIT, :] = q_buf[rows, cols]
                send[group, G_AT + at : G_AT + at + UNIT, :] = g
                product.append(g.astype(jnp.float32) * o_buf[rows, cols].astype(jnp.float32))
        own = slice(group * HEAD_WIDTH, (group + 1) * HEAD_WIDTH)
        send[group, K_AT : K_AT + TOK, :] = k_buf[:, own]
        send[group, V_AT : V_AT + TOK, :] = v_buf[:, own]
        for n, rows in enumerate((pl.ds(Q_AT, G_AT), pl.ds(G_AT, X_AT - G_AT))):
            departures.append(
                pltpu.make_async_copy(
                    send.at[group, rows], out_ref.at[group, rows], sem.at[group, n]
                )
            )
            departures[-1].start()
        delta = jnp.sum(jnp.concatenate(product, axis=0).T, axis=0, keepdims=True)
        delta = jnp.concatenate([delta[:, t * 128 : (t + 1) * 128] for t in range(6)], axis=0)
        high = delta.astype(jnp.bfloat16).astype(jnp.float32)
        extra = jnp.concatenate([high, delta - high, tail], axis=0)
        extras[group] = extra.astype(jnp.bfloat16)
    departures.append(
        pltpu.make_async_copy(extras, out_ref.at[:, pl.ds(X_AT, 16)], extra_sem.at[0])
    )
    departures[-1].start()
    for copy in departures:
        copy.wait()


def attention_kernel(
    pay_ref, out_ref, extra_ref, start_ref, first_ref, reach_ref, dk_ref, dv_ref
):
    scale = 1.0 / math.sqrt(HEAD_WIDTH)
    to_exp2 = scale * math.log2(math.e)
    dk_ref[...] = jnp.zeros_like(dk_ref)
    dv_ref[...] = jnp.zeros_like(dv_ref)
    for b in range(BLOCKS):
        extra_ref[b] = pay_ref[b, X_AT : X_AT + 16, :].astype(jnp.float32)
    docs = jnp.concatenate([extra_ref[b, 12:15, :] for b in range(BLOCKS)], axis=0)
    starts = jnp.zeros_like(docs)
    for d in range(1, DOCS):
        before = 0.5 * jnp.sum(jnp.where(docs < d, 1.0, 0.0), keepdims=True)
        starts = jnp.where(docs == d, before, starts)
    for b in range(BLOCKS):
        own = starts[UNITS * b : UNITS * (b + 1)]
        start_ref[b] = jnp.concatenate([own, own, own[:2]], axis=0)
        first_ref[b] = jnp.min(own).astype(jnp.int32)
        chunk_at = b * TOK + UNIT * lax.broadcasted_iota(jnp.int32, own.shape, 0)
        reach_ref[b] = jnp.max(chunk_at.astype(jnp.float32) - own).astype(jnp.int32)

    def case_of(i):
        unit = first_ref[i] // UNIT
        first_block = unit // UNITS
        is_short = (i > 0) & (reach_ref[i] <= SHORT - UNIT) & (first_block < i)
        return i - first_block + 1, unit % UNITS, is_short

    def chunks_of(i, count, skip=0, short=False, over=False):
        start3 = start_ref[i].astype(jnp.int32)
        delta6 = extra_ref[i, 0:6, :] + extra_ref[i, 6:12, :]
        low = i - count + 1
        row0 = pl.multiple_of(low * TOK, TOK)
        keys = pay_ref[pl.ds(low, count), K_AT : K_AT + TOK, :].reshape(count * TOK, HEAD_WIDTH)
        values = pay_ref[pl.ds(low, count), V_AT : V_AT + TOK, :].reshape(
            count * TOK, HEAD_WIDTH
        )
        token = lax.broadcasted_iota(jnp.int32, (UNIT, LANES), 1) % UNIT
        causal = lax.broadcasted_iota(jnp.int32, (UNIT, LANES), 0) <= token

        def load(t, at):
            return pay_ref[i, at + t * LANES : at + (t + 1) * LANES, :]

        def end(t):
            return (count - 1) * TOK + (t + 1) * UNIT

        def begin(t):
            ended = over and t > skip
            return end(t) - SHORT if short or ended else skip * UNIT

        def pieces(t):
            edges = list(range(begin(t), end(t), TOK)) + [end(t)]
            return [slice(p - begin(t), q - begin(t)) for p, q in zip(edges, edges[1:])]

        def scores_of(t):
            return dot(keys[begin(t) : end(t)], load(t, Q_AT), NT)

        def prob_grad_of(t):
            return dot(values[begin(t) : end(t)], load(t, G_AT), NT)

        def weigh(t, scores):
            start = jnp.concatenate([start3[t : t + 1]] * 2, axis=1) - (low * TOK + begin(t))
            parts = []
            for piece in pieces(t):
                rows = piece.stop - piece.start
                key_row = lax.broadcasted_iota(jnp.int32, (rows, LANES), 0)
                part = jnp.where(key_row >= start - piece.start, scores[piece], -1e30)
                if piece.stop == end(t) - begin(t):
                    edge = jnp.where(causal, part[rows - UNIT :], -1e30)
                    part = jnp.concatenate([part[: rows - UNIT], edge], axis=0) if rows > UNIT else edge
                top = jnp.max(part, axis=0, keepdims=True) * to_exp2
                weights = jnp.exp2(part * to_exp2 - top)
                parts.append((weights, top, jnp.sum(weights, axis=0, keepdims=True)))
            return parts

        def factors(parts):
            top = functools.reduce(jnp.maximum, [part[1] for part in parts])
            shares = [jnp.exp2(part[1] - top) for part in parts]
            total = functools.reduce(
                jnp.add, [share * part[2] for share, part in zip(shares, parts)]
            )
            inverse = 1.0 / total
            return [share * inverse for share in shares]

        def grads(t, parts, prob_grad):
            delta = jnp.concatenate(
                [delta6[2 * t : 2 * t + 1], delta6[2 * t + 1 : 2 * t + 2]], axis=1
            )
            low_probs, score_grads = [], []
            for piece, part, factor in zip(pieces(t), parts, factors(parts)):
                probs = part[0] * factor
                low_probs.append(probs.astype(jnp.bfloat16))
                score_grads.append((probs * (prob_grad[piece] - delta)).astype(jnp.bfloat16))
            if len(parts) == 1:
                return low_probs[0], score_grads[0]
            return jnp.concatenate(low_probs, axis=0), jnp.concatenate(score_grads, axis=0)

        def finish(t, probs, score_grad):
            at = pl.ds(pl.multiple_of(row0 + begin(t), UNIT), end(t) - begin(t))
            dv_ref[at] += dot(probs, load(t, G_AT), NN)
            dk_ref[at] += dot(score_grad, load(t, Q_AT), NN)
            dq = dot(keys[begin(t) : end(t)], score_grad, TN) * scale
            dq = dq.T.astype(jnp.bfloat16)
            for h in range(GROUP):
                at = h * TOK + t * UNIT
                out_ref[i, at : at + UNIT, :] = dq[h * UNIT : (h + 1) * UNIT]

        def chunk(t):
            return tuple(
                functools.partial(step, t)
                for step in (scores_of, prob_grad_of, weigh, grads, finish)
            )

        return [chunk(t) for t in range(UNITS)]

    def run(chunks):
        count = len(chunks)
        s, d, w, g = {}, {}, {}, {}

        def scores_of(n):
            s[n] = chunks[n][0]()

        def grads(n):
            g[n] = chunks[n][3](w.pop(n), d.pop(n))

        scores_of(0)
        scores_of(1)
        for n in range(count):
            if n + 2 < count:
                scores_of(n + 2)
            w[n] = chunks[n][2](s.pop(n))
            if n > 1:
                chunks[n - 2][4](*g.pop(n - 2))
            if n > 0:
                grads(n - 1)
            d[n] = chunks[n][1]()
        chunks[-2][4](*g.pop(count - 2))
        grads(count - 1)
        chunks[-1][4](*g.pop(count - 1))

    def two_blocks(p, carry):
        one, two = 2 * p, 2 * p + 1
        count1, skip1, short1 = case_of(one)
        count2, skip2, short2 = case_of(two)
        long1 = jnp.logical_not(short1)
        goes_on = (count2 == count1 + 1) & ((count1 == 1) | ((count1 == 3) & (skip1 == skip2)))
        goes_on = goes_on & long1 & jnp.logical_not(short2)
        then_short = short2 & (short1 | (count1 == 1) | (count1 == MOST_BLOCKS))

        @pl.when(goes_on)
        def _():
            for skip in range(UNITS):

                @pl.when(skip2 == skip)
                def _(skip=skip):
                    pl.when(count1 == 1)(
                        lambda: run(chunks_of(one, 1) + chunks_of(two, 2, skip))
                    )
                    pl.when(count1 == 3)(
                        lambda: run(chunks_of(one, 3, skip) + chunks_of(two, 4, skip))
                    )

        @pl.when(then_short)
        def _():
            def both(first):
                run(first + chunks_of(two, 2, short=True))

            pl.when(short1)(lambda: both(chunks_of(one, 2, short=True)))

            @pl.when(long1)
            def _():
                pl.when(count1 == 1)(lambda: both(chunks_of(one, 1)))
                for skip in range(UNITS):
                    pl.when((count1 == MOST_BLOCKS) & (skip1 == skip))(
                        lambda skip=skip: both(chunks_of(one, MOST_BLOCKS, skip, over=True))
                    )

        @pl.when(jnp.logical_not(goes_on | then_short))
        def _():
            def one_block(i, carry):
                count, skip, short = case_of(i)
                pl.when(short)(lambda: run(chunks_of(i, 2, short=True)))

                @pl.when(jnp.logical_not(short))
                def _():
                    for value in range(1, MOST_BLOCKS + 1):
                        pl.when(count == value)(lambda value=value: run(chunks_of(i, value)))

                return carry

            lax.fori_loop(one, two + 1, one_block, 0)

        return carry

    lax.fori_loop(0, BLOCKS // 2, two_blocks, 0)
    at = GROUP * TOK
    for b in range(BLOCKS):
        own = slice(b * TOK, (b + 1) * TOK)
        out_ref[b, at : at + TOK, :] = (dk_ref[own] * scale).astype(jnp.bfloat16)
        out_ref[b, at + TOK : at + 2 * TOK, :] = dv_ref[own].astype(jnp.bfloat16)


def unpack_kernel(back_ref, dq_ref, dk_ref, dv_ref, dq_buf, dk_buf, dv_buf, sem):
    copies = []
    for part in range(UNPACK_PARTS):
        size = TOK // UNPACK_PARTS
        rows = slice(part * size, (part + 1) * size)
        for group in range(KEY_VALUE_HEADS):
            for h in range(GROUP):
                head = group * GROUP + h
                at = h * TOK + part * size
                cols = slice(head * HEAD_WIDTH, (head + 1) * HEAD_WIDTH)
                dq_buf[rows, cols] = back_ref[group, at : at + size, :]
            cols = slice(group * HEAD_WIDTH, (group + 1) * HEAD_WIDTH)
            for n, buf in enumerate((dk_buf, dv_buf)):
                at = (GROUP + n) * TOK + part * size
                buf[rows, cols] = back_ref[group, at : at + size, :]
        for n, (buf, ref) in enumerate(((dq_buf, dq_ref), (dk_buf, dk_ref), (dv_buf, dv_ref))):
            copies.append(pltpu.make_async_copy(buf.at[rows], ref.at[rows], sem.at[part, n]))
            copies[-1].start()
    for copy in copies:
        copy.wait()


def local(queries, keys, values, outputs, output_gradient, doc_ids):
    hbm = pl.BlockSpec(memory_space=pltpu.HBM)
    packed = pl.pallas_call(
        pack_kernel,
        in_specs=[hbm] * 6,
        out_specs=hbm,
        out_shape=jax.ShapeDtypeStruct((KEY_VALUE_HEADS, SEND_ROWS, 128), jnp.bfloat16),
        scratch_shapes=[
            pltpu.VMEM(queries.shape, jnp.bfloat16),
            pltpu.VMEM(keys.shape, jnp.bfloat16),
            pltpu.VMEM(values.shape, jnp.bfloat16),
            pltpu.VMEM(outputs.shape, jnp.bfloat16),
            pltpu.VMEM(output_gradient.shape, jnp.bfloat16),
            pltpu.VMEM((1, TOK), jnp.int32),
            pltpu.VMEM((KEY_VALUE_HEADS, X_AT, 128), jnp.bfloat16),
            pltpu.VMEM((KEY_VALUE_HEADS, 16, 128), jnp.bfloat16),
            pltpu.SemaphoreType.DMA((3, KEY_VALUE_HEADS)),
            pltpu.SemaphoreType.DMA((3,)),
            pltpu.SemaphoreType.DMA((KEY_VALUE_HEADS, 2)),
            pltpu.SemaphoreType.DMA((1,)),
        ],
        compiler_params=pltpu.CompilerParams(vmem_limit_bytes=62 * 2**20),
        name="pack",
    )(queries, keys, values, outputs, output_gradient, doc_ids.reshape(1, TOK))
    payload = lax.all_to_all(packed, "blk", 0, 0, tiled=True)
    result = pl.pallas_call(
        attention_kernel,
        out_shape=jax.ShapeDtypeStruct((BLOCKS, BACK_ROWS, 128), jnp.bfloat16),
        scratch_shapes=[
            pltpu.VMEM((BLOCKS, 16, 128), jnp.float32),
            pltpu.VMEM((BLOCKS, 8, 128), jnp.float32),
            pltpu.SMEM((BLOCKS,), jnp.int32),
            pltpu.SMEM((BLOCKS,), jnp.int32),
            pltpu.VMEM((BLOCKS * TOK, HEAD_WIDTH), jnp.float32),
            pltpu.VMEM((BLOCKS * TOK, HEAD_WIDTH), jnp.float32),
        ],
        compiler_params=pltpu.CompilerParams(vmem_limit_bytes=32 * 2**20),
        name="attention",
    )(payload)
    back = lax.all_to_all(result, "blk", 0, 0, tiled=True)
    return pl.pallas_call(
        unpack_kernel,
        in_specs=[pl.BlockSpec(memory_space=pltpu.VMEM)],
        out_specs=[hbm] * 3,
        out_shape=[
            jax.ShapeDtypeStruct(queries.shape, jnp.bfloat16),
            jax.ShapeDtypeStruct(keys.shape, jnp.bfloat16),
            jax.ShapeDtypeStruct(values.shape, jnp.bfloat16),
        ],
        scratch_shapes=[
            pltpu.VMEM(queries.shape, jnp.bfloat16),
            pltpu.VMEM(keys.shape, jnp.bfloat16),
            pltpu.VMEM(values.shape, jnp.bfloat16),
            pltpu.SemaphoreType.DMA((UNPACK_PARTS, 3)),
        ],
        compiler_params=pltpu.CompilerParams(vmem_limit_bytes=32 * 2**20),
        name="unpack",
    )(back)


def solution(mesh):
    rows = P(("dp", "blk"), None)
    return jax.shard_map(
        local,
        mesh=mesh,
        in_specs=(rows, rows, rows, rows, rows, P(("dp", "blk"))),
        out_specs=(rows, rows, rows),
        check_vma=False,
    )
```

```python
import functools
import math

import jax
import jax.numpy as jnp
from jax import lax
from jax.experimental import pallas as pl
from jax.experimental.pallas import tpu as pltpu
from jax.sharding import PartitionSpec as P

QUERY_HEADS = 32
KEY_VALUE_HEADS = 8
HEAD_WIDTH = 128
GROUP = QUERY_HEADS // KEY_VALUE_HEADS
DOCS = 8
TOK = 192
BLOCKS = 8
MOST_BLOCKS = 5
UNIT = 64
UNITS = TOK // UNIT
LANES = GROUP * UNIT
UNPACK_PARTS = 4
SHORT = 3 * UNIT
Q_AT = 0
G_AT = GROUP * TOK
K_AT = 2 * GROUP * TOK
V_AT = K_AT + TOK
X_AT = V_AT + TOK
SEND_ROWS = X_AT + 16
BACK_ROWS = (GROUP + 2) * TOK
NT = (((1,), (1,)), ((), ()))
TN = (((0,), (0,)), ((), ()))
NN = (((1,), (0,)), ((), ()))


def dot(a, b, dims):
    return lax.dot_general(a, b, dims, preferred_element_type=jnp.float32)


def pack_kernel(
    q_ref, k_ref, v_ref, o_ref, g_ref, doc_ref, out_ref, q_buf, k_buf, v_buf, o_buf, g_buf, doc_buf, send, extras, in_sem, kv_sem, sem, extra_sem
):
    whole = [
        pltpu.make_async_copy(k_ref, k_buf, kv_sem.at[0]),
        pltpu.make_async_copy(v_ref, v_buf, kv_sem.at[1]),
        pltpu.make_async_copy(doc_ref, doc_buf, kv_sem.at[2]),
    ]
    arrivals = []
    for group in range(KEY_VALUE_HEADS):
        cols = slice(group * GROUP * HEAD_WIDTH, (group + 1) * GROUP * HEAD_WIDTH)
        arrivals.append(
            [
                pltpu.make_async_copy(ref.at[:, cols], buf.at[:, cols], in_sem.at[n, group])
                for n, (ref, buf) in enumerate(((g_ref, g_buf), (o_ref, o_buf), (q_ref, q_buf)))
            ]
        )
        for copy in arrivals[group]:
            copy.start()
        if group == 0:
            for copy in whole:
                copy.start()
    departures = []

    def depart(group, n, first, last):
        rows = pl.ds(first, last - first)
        departures.append(
            pltpu.make_async_copy(send.at[group, rows], out_ref.at[group, rows], sem.at[group, n])
        )
        departures[-1].start()

    for group in range(KEY_VALUE_HEADS):
        for copy in arrivals[group]:
            copy.wait()
        product = []
        for t in range(UNITS):
            rows = slice(t * UNIT, (t + 1) * UNIT)
            for h in range(GROUP):
                head = group * GROUP + h
                cols = slice(head * HEAD_WIDTH, (head + 1) * HEAD_WIDTH)
                at = t * LANES + h * UNIT
                g = g_buf[rows, cols]
                send[group, Q_AT + at : Q_AT + at + UNIT, :] = q_buf[rows, cols]
                send[group, G_AT + at : G_AT + at + UNIT, :] = g
                product.append(g.astype(jnp.float32) * o_buf[rows, cols].astype(jnp.float32))
        depart(group, 0, Q_AT, G_AT)
        depart(group, 1, G_AT, K_AT)
        if group == 0:
            for copy in whole:
                copy.wait()
            doc = doc_buf[...].astype(jnp.float32)
            tail = [doc[:, t * UNIT : (t + 1) * UNIT] for t in range(UNITS)]
            tail = [jnp.concatenate([part, part], axis=1) for part in tail]
            tail = jnp.concatenate(tail + [jnp.zeros((1, 128), jnp.float32)], axis=0)
        own = slice(group * HEAD_WIDTH, (group + 1) * HEAD_WIDTH)
        send[group, K_AT : K_AT + TOK, :] = k_buf[:, own]
        send[group, V_AT : V_AT + TOK, :] = v_buf[:, own]
        depart(group, 2, K_AT, X_AT)
        delta = jnp.sum(jnp.concatenate(product, axis=0).T, axis=0, keepdims=True)
        delta = jnp.concatenate([delta[:, t * 128 : (t + 1) * 128] for t in range(6)], axis=0)
        high = delta.astype(jnp.bfloat16).astype(jnp.float32)
        extra = jnp.concatenate([high, delta - high, tail], axis=0)
        extras[group] = extra.astype(jnp.bfloat16)
    departures.append(
        pltpu.make_async_copy(extras, out_ref.at[:, pl.ds(X_AT, 16)], extra_sem.at[0])
    )
    departures[-1].start()
    for copy in departures:
        copy.wait()


def attention_kernel(
    pay_ref, out_ref, extra_ref, start_ref, first_ref, reach_ref, dk_ref, dv_ref
):
    scale = 1.0 / math.sqrt(HEAD_WIDTH)
    to_exp2 = scale * math.log2(math.e)
    dk_ref[...] = jnp.zeros_like(dk_ref)
    dv_ref[...] = jnp.zeros_like(dv_ref)
    for b in range(BLOCKS):
        extra_ref[b] = pay_ref[b, X_AT : X_AT + 16, :].astype(jnp.float32)
    docs = jnp.concatenate([extra_ref[b, 12:15, :] for b in range(BLOCKS)], axis=0)
    starts = jnp.zeros_like(docs)
    for d in range(1, DOCS):
        before = 0.5 * jnp.sum(jnp.where(docs < d, 1.0, 0.0), keepdims=True)
        starts = jnp.where(docs == d, before, starts)
    for b in range(BLOCKS):
        own = starts[UNITS * b : UNITS * (b + 1)]
        start_ref[b] = jnp.concatenate([own, own, own[:2]], axis=0)
        first_ref[b] = jnp.min(own).astype(jnp.int32)
        chunk_at = b * TOK + UNIT * lax.broadcasted_iota(jnp.int32, own.shape, 0)
        reach_ref[b] = jnp.max(chunk_at.astype(jnp.float32) - own).astype(jnp.int32)

    def case_of(i):
        unit = first_ref[i] // UNIT
        first_block = unit // UNITS
        is_short = (i > 0) & (reach_ref[i] <= SHORT - UNIT) & (first_block < i)
        return i - first_block + 1, unit % UNITS, is_short

    def chunks_of(i, count, skip=0, short=False, over=False):
        start3 = start_ref[i].astype(jnp.int32)
        delta6 = extra_ref[i, 0:6, :] + extra_ref[i, 6:12, :]
        low = i - count + 1
        row0 = pl.multiple_of(low * TOK, TOK)
        keys = pay_ref[pl.ds(low, count), K_AT : K_AT + TOK, :].reshape(count * TOK, HEAD_WIDTH)
        values = pay_ref[pl.ds(low, count), V_AT : V_AT + TOK, :].reshape(
            count * TOK, HEAD_WIDTH
        )
        token = lax.broadcasted_iota(jnp.int32, (UNIT, LANES), 1) % UNIT
        causal = lax.broadcasted_iota(jnp.int32, (UNIT, LANES), 0) <= token

        def load(t, at):
            return pay_ref[i, at + t * LANES : at + (t + 1) * LANES, :]

        def end(t):
            return (count - 1) * TOK + (t + 1) * UNIT

        def begin(t):
            ended = over and t > skip
            return end(t) - SHORT if short or ended else skip * UNIT

        def pieces(t):
            edges = list(range(begin(t), end(t), TOK)) + [end(t)]
            return [slice(p - begin(t), q - begin(t)) for p, q in zip(edges, edges[1:])]

        def scores_of(t):
            return dot(keys[begin(t) : end(t)], load(t, Q_AT), NT)

        def prob_grad_of(t):
            return dot(values[begin(t) : end(t)], load(t, G_AT), NT)

        def weigh(t, scores):
            start = jnp.concatenate([start3[t : t + 1]] * 2, axis=1) - (low * TOK + begin(t))
            parts = []
            for piece in pieces(t):
                rows = piece.stop - piece.start
                key_row = lax.broadcasted_iota(jnp.int32, (rows, LANES), 0)
                part = jnp.where(key_row >= start - piece.start, scores[piece], -1e30)
                if piece.stop == end(t) - begin(t):
                    edge = jnp.where(causal, part[rows - UNIT :], -1e30)
                    part = jnp.concatenate([part[: rows - UNIT], edge], axis=0) if rows > UNIT else edge
                top = jnp.max(part, axis=0, keepdims=True) * to_exp2
                weights = jnp.exp2(part * to_exp2 - top)
                parts.append((weights, top, jnp.sum(weights, axis=0, keepdims=True)))
            return parts

        def factors(parts):
            top = functools.reduce(jnp.maximum, [part[1] for part in parts])
            shares = [jnp.exp2(part[1] - top) for part in parts]
            total = functools.reduce(
                jnp.add, [share * part[2] for share, part in zip(shares, parts)]
            )
            inverse = 1.0 / total
            return [share * inverse for share in shares]

        def grads(t, parts, prob_grad):
            delta = jnp.concatenate(
                [delta6[2 * t : 2 * t + 1], delta6[2 * t + 1 : 2 * t + 2]], axis=1
            )
            low_probs, score_grads = [], []
            for piece, part, factor in zip(pieces(t), parts, factors(parts)):
                probs = part[0] * factor
                low_probs.append(probs.astype(jnp.bfloat16))
                score_grads.append((probs * (prob_grad[piece] - delta)).astype(jnp.bfloat16))
            if len(parts) == 1:
                return low_probs[0], score_grads[0]
            return jnp.concatenate(low_probs, axis=0), jnp.concatenate(score_grads, axis=0)

        def finish(t, probs, score_grad):
            at = pl.ds(pl.multiple_of(row0 + begin(t), UNIT), end(t) - begin(t))
            dv_ref[at] += dot(probs, load(t, G_AT), NN)
            dk_ref[at] += dot(score_grad, load(t, Q_AT), NN)
            dq = dot(keys[begin(t) : end(t)], score_grad, TN) * scale
            dq = dq.T.astype(jnp.bfloat16)
            for h in range(GROUP):
                at = h * TOK + t * UNIT
                out_ref[i, at : at + UNIT, :] = dq[h * UNIT : (h + 1) * UNIT]

        def chunk(t):
            return tuple(
                functools.partial(step, t)
                for step in (scores_of, prob_grad_of, weigh, grads, finish)
            )

        return [chunk(t) for t in range(UNITS)]

    def run(chunks):
        count = len(chunks)
        s, d, w, g = {}, {}, {}, {}

        def scores_of(n):
            s[n] = chunks[n][0]()

        def grads(n):
            g[n] = chunks[n][3](w.pop(n), d.pop(n))

        scores_of(0)
        scores_of(1)
        for n in range(count):
            if n + 2 < count:
                scores_of(n + 2)
            w[n] = chunks[n][2](s.pop(n))
            if n > 1:
                chunks[n - 2][4](*g.pop(n - 2))
            if n > 0:
                grads(n - 1)
            d[n] = chunks[n][1]()
        chunks[-2][4](*g.pop(count - 2))
        grads(count - 1)
        chunks[-1][4](*g.pop(count - 1))

    def two_blocks(p, carry):
        one, two = 2 * p, 2 * p + 1
        count1, skip1, short1 = case_of(one)
        count2, skip2, short2 = case_of(two)
        long1 = jnp.logical_not(short1)
        goes_on = (count2 == count1 + 1) & ((count1 == 1) | ((count1 == 3) & (skip1 == skip2)))
        goes_on = goes_on & long1 & jnp.logical_not(short2)
        then_short = short2 & (short1 | (count1 == 1) | (count1 == MOST_BLOCKS))

        @pl.when(goes_on)
        def _():
            for skip in range(UNITS):

                @pl.when(skip2 == skip)
                def _(skip=skip):
                    pl.when(count1 == 1)(
                        lambda: run(chunks_of(one, 1) + chunks_of(two, 2, skip))
                    )
                    pl.when(count1 == 3)(
                        lambda: run(chunks_of(one, 3, skip) + chunks_of(two, 4, skip))
                    )

        @pl.when(then_short)
        def _():
            def both(first):
                run(first + chunks_of(two, 2, short=True))

            pl.when(short1)(lambda: both(chunks_of(one, 2, short=True)))

            @pl.when(long1)
            def _():
                pl.when(count1 == 1)(lambda: both(chunks_of(one, 1)))
                for skip in range(UNITS):
                    pl.when((count1 == MOST_BLOCKS) & (skip1 == skip))(
                        lambda skip=skip: both(chunks_of(one, MOST_BLOCKS, skip, over=True))
                    )

        @pl.when(jnp.logical_not(goes_on | then_short))
        def _():
            def one_block(i, carry):
                count, skip, short = case_of(i)
                pl.when(short)(lambda: run(chunks_of(i, 2, short=True)))

                @pl.when(jnp.logical_not(short))
                def _():
                    for value in range(1, MOST_BLOCKS + 1):
                        pl.when(count == value)(lambda value=value: run(chunks_of(i, value)))

                return carry

            lax.fori_loop(one, two + 1, one_block, 0)

        return carry

    lax.fori_loop(0, BLOCKS // 2, two_blocks, 0)
    at = GROUP * TOK
    for b in range(BLOCKS):
        own = slice(b * TOK, (b + 1) * TOK)
        out_ref[b, at : at + TOK, :] = (dk_ref[own] * scale).astype(jnp.bfloat16)
        out_ref[b, at + TOK : at + 2 * TOK, :] = dv_ref[own].astype(jnp.bfloat16)


def unpack_kernel(back_ref, dq_ref, dk_ref, dv_ref, dq_buf, dk_buf, dv_buf, sem):
    copies = []
    for part in range(UNPACK_PARTS):
        size = TOK // UNPACK_PARTS
        rows = slice(part * size, (part + 1) * size)
        for group in range(KEY_VALUE_HEADS):
            for h in range(GROUP):
                head = group * GROUP + h
                at = h * TOK + part * size
                cols = slice(head * HEAD_WIDTH, (head + 1) * HEAD_WIDTH)
                dq_buf[rows, cols] = back_ref[group, at : at + size, :]
            cols = slice(group * HEAD_WIDTH, (group + 1) * HEAD_WIDTH)
            for n, buf in enumerate((dk_buf, dv_buf)):
                at = (GROUP + n) * TOK + part * size
                buf[rows, cols] = back_ref[group, at : at + size, :]
        for n, (buf, ref) in enumerate(((dq_buf, dq_ref), (dk_buf, dk_ref), (dv_buf, dv_ref))):
            copies.append(pltpu.make_async_copy(buf.at[rows], ref.at[rows], sem.at[part, n]))
            copies[-1].start()
    for copy in copies:
        copy.wait()


def local(queries, keys, values, outputs, output_gradient, doc_ids):
    hbm = pl.BlockSpec(memory_space=pltpu.HBM)
    packed = pl.pallas_call(
        pack_kernel,
        in_specs=[hbm] * 6,
        out_specs=hbm,
        out_shape=jax.ShapeDtypeStruct((KEY_VALUE_HEADS, SEND_ROWS, 128), jnp.bfloat16),
        scratch_shapes=[
            pltpu.VMEM(queries.shape, jnp.bfloat16),
            pltpu.VMEM(keys.shape, jnp.bfloat16),
            pltpu.VMEM(values.shape, jnp.bfloat16),
            pltpu.VMEM(outputs.shape, jnp.bfloat16),
            pltpu.VMEM(output_gradient.shape, jnp.bfloat16),
            pltpu.VMEM((1, TOK), jnp.int32),
            pltpu.VMEM((KEY_VALUE_HEADS, X_AT, 128), jnp.bfloat16),
            pltpu.VMEM((KEY_VALUE_HEADS, 16, 128), jnp.bfloat16),
            pltpu.SemaphoreType.DMA((3, KEY_VALUE_HEADS)),
            pltpu.SemaphoreType.DMA((3,)),
            pltpu.SemaphoreType.DMA((KEY_VALUE_HEADS, 3)),
            pltpu.SemaphoreType.DMA((1,)),
        ],
        compiler_params=pltpu.CompilerParams(vmem_limit_bytes=62 * 2**20),
        name="pack",
    )(queries, keys, values, outputs, output_gradient, doc_ids.reshape(1, TOK))
    payload = lax.all_to_all(packed, "blk", 0, 0, tiled=True)
    result = pl.pallas_call(
        attention_kernel,
        out_shape=jax.ShapeDtypeStruct((BLOCKS, BACK_ROWS, 128), jnp.bfloat16),
        scratch_shapes=[
            pltpu.VMEM((BLOCKS, 16, 128), jnp.float32),
            pltpu.VMEM((BLOCKS, 8, 128), jnp.float32),
            pltpu.SMEM((BLOCKS,), jnp.int32),
            pltpu.SMEM((BLOCKS,), jnp.int32),
            pltpu.VMEM((BLOCKS * TOK, HEAD_WIDTH), jnp.float32),
            pltpu.VMEM((BLOCKS * TOK, HEAD_WIDTH), jnp.float32),
        ],
        compiler_params=pltpu.CompilerParams(vmem_limit_bytes=32 * 2**20),
        name="attention",
    )(payload)
    back = lax.all_to_all(result, "blk", 0, 0, tiled=True)
    return pl.pallas_call(
        unpack_kernel,
        in_specs=[pl.BlockSpec(memory_space=pltpu.VMEM)],
        out_specs=[hbm] * 3,
        out_shape=[
            jax.ShapeDtypeStruct(queries.shape, jnp.bfloat16),
            jax.ShapeDtypeStruct(keys.shape, jnp.bfloat16),
            jax.ShapeDtypeStruct(values.shape, jnp.bfloat16),
        ],
        scratch_shapes=[
            pltpu.VMEM(queries.shape, jnp.bfloat16),
            pltpu.VMEM(keys.shape, jnp.bfloat16),
            pltpu.VMEM(values.shape, jnp.bfloat16),
            pltpu.SemaphoreType.DMA((UNPACK_PARTS, 3)),
        ],
        compiler_params=pltpu.CompilerParams(vmem_limit_bytes=32 * 2**20),
        name="unpack",
    )(back)


def solution(mesh):
    rows = P(("dp", "blk"), None)
    return jax.shard_map(
        local,
        mesh=mesh,
        in_specs=(rows, rows, rows, rows, rows, P(("dp", "blk"))),
        out_specs=(rows, rows, rows),
        check_vma=False,
    )
```
